32 devices in a mesh: wide: 8 (over z, y), tp: 4 (over x, core).
Axes of the slice: x: 2, y: 2, z: 4, core: 2. Of those that a mesh axis runs over, the one named last changes fastest.
Arguments:
- block_input: bfloat16 [16384, 1024], P(('wide', 'tp')), may hold values from -6 to 6
- mix_gain: float32 [1024], replicated, may hold values from 0.5 to 1.5
- query_weight: bfloat16 [1024, 512], P('wide', 'tp'), may hold values from -0.1875 to 0.1875
- zx_weight: bfloat16 [1024, 2, 1536], P('wide', None, 'tp'), may hold values from -0.1875 to 0.1875
- step_weight: bfloat16 [1024, 24], P('wide', 'tp'), may hold values from -0.1875 to 0.1875
- shared_weight: bfloat16 [1024, 4, 128], P('wide'), may hold values from -0.1875 to 0.1875
- conv_inner: float32 [4, 1536], P(None, 'tp'), may hold values from -3 to 3
- conv_shared: float32 [4, 2, 128], replicated, may hold values from -3 to 3
- step_bias: float32 [24], P('tp'), may hold values from -6 to -1
- decay_log: float32 [24], P('tp'), may hold values from 0 to 2.5
- skip_gain: float32 [24], P('tp'), may hold values from 0.5 to 1.5
- attention_out: bfloat16 [512, 1024], P('tp', 'wide'), may hold values from -2 to 2
- mamba_out: bfloat16 [1536, 1024], P('tp', 'wide'), may hold values from -0.3125 to 0.3125
- feed_gain: float32 [1024], replicated, may hold values from 0.5 to 1.5
- gate_up: bfloat16 [1024, 2, 2048], P('wide', None, 'tp'), may hold values from -0.1875 to 0.1875
- down_weight: bfloat16 [2048, 1024], P('tp', 'wide'), may hold values from -0.125 to 0.125
- output_grad: bfloat16 [16384, 1024], P(('wide', 'tp')), may hold values from -6 to 6
Outputs:
- block_output: bfloat16 [16384, 1024], P(('wide', 'tp'))
- input_grad: bfloat16 [16384, 1024], P(('wide', 'tp'))
- mix_gain_grad: float32 [1024], replicated
- query_grad: float32 [1024, 512], P('wide', 'tp')
- zx_grad: float32 [1024, 2, 1536], P('wide', None, 'tp')
- step_grad: float32 [1024, 24], P('wide', 'tp')
- shared_grad: float32 [1024, 4, 128], P('wide')
- conv_inner_grad: float32 [4, 1536], P(None, 'tp')
- conv_shared_grad: float32 [4, 2, 128], replicated
- step_bias_grad: float32 [24], P('tp')
- decay_log_grad: float32 [24], P('tp')
- skip_gain_grad: float32 [24], P('tp')
- attention_out_grad: float32 [512, 1024], P('tp', 'wide')
- mamba_out_grad: float32 [1536, 1024], P('tp', 'wide')
- feed_gain_grad: float32 [1024], replicated
- gate_up_grad: float32 [1024, 2, 2048], P('wide', None, 'tp')
- down_grad: float32 [2048, 1024], P('tp', 'wide')
The draws below stay inside these ranges and needn't reach their ends.
All inputs are finite; a program needn't handle non-finite values.
Results may differ from the reference program's by a relative error of at most 0.024.
Values may be sent and summed in bfloat16 or wider, within the bound.
A program may use at most 192 MiB of HBM per device.

```python
import jax
import jax.numpy as jnp
from jax import lax

D = 1024
HEADS = 8
KV_HEADS = 2
HEAD_DIM = 64
MHEADS = 24
MHEAD_DIM = 64
STATE = 128
CONV = 4
FF = 2048
SEQS = 1
SEQ_LEN = 2048
SPAN = 128
QBLOCK = 512
TOKENS = 16384
DSSM = 1536
QCOLS = 512
N_TP = 4


def steps_of(stream_key, dims, split, least, high):
    loudness = 1.0
    for dim, blocks in split:
        draws = jax.random.uniform(jax.random.fold_in(jax.random.fold_in(stream_key, 6), dim), (blocks,), jnp.float32, least / len(split), high / len(split))
        loudness = loudness * jnp.repeat(jnp.exp(draws), dims[dim] // blocks).reshape((-1,) + (1,) * (len(dims) - 1 - dim))
    return loudness


def gaussian(stream_key, extent, deviation, reach, cuts=(), kind=jnp.bfloat16):
    entries = deviation * jax.random.normal(stream_key, extent, jnp.float32)
    if cuts:
        entries = entries * steps_of(stream_key, extent, cuts, -0.22, 0.18)
    return jnp.clip(entries, -reach, reach).astype(kind)


def setup_inputs(seed: int = 0) -> dict:
    key_of = jax.random.split(jax.random.key(seed), 18)
    return {
        "block_input": gaussian(key_of[0], (TOKENS, D), 1.0, 6.0, ((0, 32),)),
        "mix_gain": jnp.clip(1.0 + 0.1 * jax.random.normal(key_of[1], (D,), jnp.float32), 0.5, 1.5),
        "query_weight": gaussian(key_of[2], (D, QCOLS), D ** -0.5, 0.1875, ((0, 8), (1, 4))),
        "zx_weight": gaussian(key_of[3], (D, 2, DSSM), D ** -0.5, 0.1875, ((0, 8), (2, 4))),
        "step_weight": gaussian(key_of[4], (D, MHEADS), D ** -0.5, 0.1875, ((0, 8), (1, 4))),
        "shared_weight": gaussian(key_of[5], (D, 4, STATE), D ** -0.5, 0.1875, ((0, 8),)),
        "conv_inner": gaussian(key_of[6], (CONV, DSSM), CONV ** -0.5, 3.0, ((1, 4),), jnp.float32),
        "conv_shared": gaussian(key_of[7], (CONV, 2, STATE), CONV ** -0.5, 3.0, (), jnp.float32),
        "step_bias": jnp.clip(-6.0 + 5.0 * jax.random.uniform(key_of[8], (MHEADS,), jnp.float32) ** steps_of(key_of[8], (MHEADS,), ((0, 4),), -0.2, 0.2), -6.0, -1.0),
        "decay_log": jnp.clip(2.5 * jax.random.uniform(key_of[9], (MHEADS,), jnp.float32) ** steps_of(key_of[9], (MHEADS,), ((0, 4),), -0.2, 0.2), 0.0, 2.5),
        "skip_gain": jnp.clip(0.5 + 1.0 * jax.random.uniform(key_of[10], (MHEADS,), jnp.float32) ** steps_of(key_of[10], (MHEADS,), ((0, 4),), -0.2, 0.2), 0.5, 1.5),
        "attention_out": gaussian(key_of[11], (QCOLS, D), (HEAD_DIM // 8) ** -0.5, 2.0, ((0, 4), (1, 8))),
        "mamba_out": gaussian(key_of[12], (DSSM, D), (DSSM // 4) ** -0.5, 0.3125, ((0, 4), (1, 8))),
        "feed_gain": jnp.clip(1.0 + 0.1 * jax.random.normal(key_of[13], (D,), jnp.float32), 0.5, 1.5),
        "gate_up": gaussian(key_of[14], (D, 2, FF), D ** -0.5, 0.1875, ((0, 8), (2, 4))),
        "down_weight": gaussian(key_of[15], (FF, D), FF ** -0.5, 0.125, ((0, 4), (1, 8))),
        "output_grad": gaussian(key_of[16], (TOKENS, D), 1.0, 6.0, ((0, 32),)),
    }


epsilon = 1e-06
HIGHEST_PRECISION = lax.Precision.HIGHEST

@jax.custom_vjp
def low(v):
    return lax.optimization_barrier(v.astype(jnp.bfloat16)).astype(jnp.float32)

@jax.custom_vjp
def low_back(v):
    return v

def low_keep(v):
    return (low(v), None)

def low_pass(kept, grad):
    return (grad,)

def back_keep(v):
    return (v, None)

def back_low(kept, grad):
    return (low(grad),)
low.defvjp(low_keep, low_pass)
low_back.defvjp(back_keep, back_low)

def rms_norm(values, gain):
    factor = lax.rsqrt(lax.optimization_barrier(jnp.mean(values * values, axis=-1, keepdims=True)) + epsilon)
    return values * factor * gain

def causal_conv(signal, kernel):
    taps = kernel.shape[0]
    length = signal.shape[1]
    padded = jnp.pad(signal, ((0, 0), (taps - 1, 0), (0, 0)))
    result = jnp.zeros_like(signal)
    for offset in range(taps):
        result = result + padded[:, offset:offset + length, :] * kernel[offset]
    return result

def ssd_scan(inner_vals, step_sizes, decay_rate, key_rows, query_rows, block):
    seq_count, length, head_count, head_width = inner_vals.shape
    span_count = length // block
    span_inputs = inner_vals.reshape(seq_count, span_count, block, head_count, head_width)
    span_steps = step_sizes.reshape(seq_count, span_count, block, head_count)
    span_keys = key_rows.reshape(seq_count, span_count, block, -1)
    span_queries = query_rows.reshape(seq_count, span_count, block, -1)
    cumulative = jnp.cumsum(span_steps * decay_rate, axis=2)
    affinity = jnp.einsum('scqn,scrn->scqr', span_queries, span_keys, precision=HIGHEST_PRECISION)
    causal = jnp.arange(block)[:, None] >= jnp.arange(block)[None, :]
    spread = cumulative[:, :, :, None, :] - cumulative[:, :, None, :, :]
    within = jnp.exp(jnp.where(causal[None, None, :, :, None], spread, -1e+30))
    mixing = affinity[..., None] * within * span_steps[:, :, None, :, :]
    intra = jnp.einsum('scqrh,scrhp->scqhp', mixing, span_inputs, precision=HIGHEST_PRECISION)
    to_end = jnp.exp(cumulative[:, :, -1:, :] - cumulative) * span_steps
    states = jnp.einsum('scqhp,scqn->schpn', span_inputs * to_end[..., None], span_keys, precision=HIGHEST_PRECISION)
    totals = jnp.exp(cumulative[:, :, -1, :])

    def advance(carried, element):
        factor, fresh = element
        return (carried * factor[:, :, None, None] + fresh, carried)
    start_state = jnp.zeros((seq_count, head_count, head_width, span_keys.shape[-1]), jnp.float32)
    _, prior = lax.scan(advance, start_state, (jnp.moveaxis(totals, 1, 0), jnp.moveaxis(states, 1, 0)))
    prior = jnp.moveaxis(prior, 0, 1)
    inter = jnp.einsum('scqn,schpn->scqhp', span_queries, prior, precision=HIGHEST_PRECISION) * jnp.exp(cumulative)[..., None]
    return (intra + inter).reshape(seq_count, length, head_count, head_width)

def mamba_mix(gate_vals, inner_raw, shared_raw, step_raw, conv_inner, conv_shared, step_bias, decay_log, skip_gain, block):
    seq_count, length, channel_count = inner_raw.shape
    head_count = step_raw.shape[-1]
    state_size = shared_raw.shape[-1]
    signal = jnp.concatenate([inner_raw, shared_raw.reshape(seq_count, length, 2 * state_size)], axis=-1)
    kernel = jnp.concatenate([conv_inner, conv_shared.reshape(conv_shared.shape[0], 2 * state_size)], axis=-1)
    convolved = jax.nn.silu(causal_conv(signal, kernel))
    inner_vals = convolved[..., :channel_count].reshape(seq_count, length, head_count, channel_count // head_count)
    key_rows = convolved[..., channel_count:channel_count + state_size]
    query_rows = convolved[..., channel_count + state_size:]
    step_sizes = jax.nn.softplus(step_raw + step_bias)
    decay_rate = -jnp.exp(decay_log)
    output = ssd_scan(inner_vals, step_sizes, decay_rate, key_rows, query_rows, block) + skip_gain[:, None] * inner_vals
    return output.reshape(seq_count, length, channel_count) * jax.nn.silu(gate_vals)

def attention(query_vals, key_vals, value_vals, block):
    seq_count, length, head_count, head_width = query_vals.shape
    scale = head_width ** (-0.5)
    key_pos = jnp.arange(length).astype(jnp.int32)

    def one_block(block_start):
        query_block = lax.dynamic_slice_in_dim(query_vals, block_start, block, 1)
        scores = low_back(jnp.einsum('sqhd,skhd->shqk', query_block, key_vals, precision=HIGHEST_PRECISION) * scale)
        query_pos = block_start + jnp.arange(block).astype(jnp.int32)
        visible = query_pos[:, None] >= key_pos[None, :]
        scores = jnp.where(visible, scores, -1e+30)
        row_max = lax.optimization_barrier(jnp.max(scores, axis=-1, keepdims=True))
        exponent = jnp.exp(scores - row_max)
        soft = low(exponent / lax.optimization_barrier(jnp.sum(exponent, axis=-1, keepdims=True)))
        return jnp.einsum('shqk,skhd->sqhd', soft, value_vals, precision=HIGHEST_PRECISION)
    starts = (jnp.arange(length // block) * block).astype(jnp.int32)
    blocks_out = lax.map(jax.checkpoint(one_block), starts)
    return jnp.moveaxis(blocks_out, 0, 1).reshape(seq_count, length, head_count, head_width)

def block_forward(inputs, mix_gain, query_weight, zx_weight, step_weight, shared_weight, conv_inner, conv_shared, step_bias, decay_log, skip_gain, attention_out, mamba_out, feed_gain, gate_up, down_weight):
    token_count = inputs.shape[0]
    seq_count = token_count // SEQ_LEN
    local_heads = HEADS // N_TP
    group_size = HEADS // KV_HEADS
    normed = low_back(low(rms_norm(inputs, mix_gain)))
    queries = low_back(low(jnp.dot(normed, query_weight, precision=HIGHEST_PRECISION)))
    shared = jnp.einsum('td,dkc->tkc', normed, shared_weight, precision=HIGHEST_PRECISION)
    keyvals = low(shared[:, 0:2].reshape(token_count, 2, KV_HEADS, HEAD_DIM))
    copies = [low_back(keyvals[:, :, owner * local_heads // group_size]) for owner in range(N_TP)]
    per_head = jnp.stack([copies[head // local_heads] for head in range(HEADS)], axis=2)
    attn = attention(queries.reshape(seq_count, SEQ_LEN, HEADS, HEAD_DIM), per_head[:, 0].reshape(seq_count, SEQ_LEN, HEADS, HEAD_DIM), per_head[:, 1].reshape(seq_count, SEQ_LEN, HEADS, HEAD_DIM), QBLOCK)
    attn = low_back(low(attn.reshape(token_count, HEADS * HEAD_DIM)))
    gate_input = low_back(jnp.einsum('td,dkc->tkc', normed, zx_weight, precision=HIGHEST_PRECISION))
    step_raw = low_back(jnp.dot(normed, step_weight, precision=HIGHEST_PRECISION))
    bc_raw = shared[:, 2:4]
    channel_width = MHEADS * MHEAD_DIM // N_TP
    head_width = MHEADS // N_TP
    pieces = []
    for owner in range(N_TP):
        channels = slice(owner * channel_width, (owner + 1) * channel_width)
        head_range = slice(owner * head_width, (owner + 1) * head_width)
        bc_copy = low_back(bc_raw)
        pieces.append(mamba_mix(gate_input[:, 0, channels].reshape(seq_count, SEQ_LEN, channel_width), gate_input[:, 1, channels].reshape(seq_count, SEQ_LEN, channel_width), bc_copy.reshape(seq_count, SEQ_LEN, 2, STATE), step_raw[:, head_range].reshape(seq_count, SEQ_LEN, head_width), conv_inner[:, channels], conv_shared, step_bias[head_range], decay_log[head_range], skip_gain[head_range], SPAN))
    gated = low_back(low(jnp.concatenate(pieces, axis=-1).reshape(token_count, MHEADS * MHEAD_DIM)))
    mixed = low_back(jnp.dot(attn, attention_out, precision=HIGHEST_PRECISION) + jnp.dot(gated, mamba_out, precision=HIGHEST_PRECISION))
    hidden_state = inputs + mixed
    normed_two = low_back(low(rms_norm(hidden_state, feed_gain)))
    gate_vals = low_back(jnp.einsum('td,dkf->tkf', normed_two, gate_up, precision=HIGHEST_PRECISION))
    hidden = low(jax.nn.silu(gate_vals[:, 0]) * gate_vals[:, 1])
    feed = low_back(jnp.dot(hidden, down_weight, precision=HIGHEST_PRECISION))
    return hidden_state + feed

def reference(block_input, mix_gain, query_weight, zx_weight, step_weight, shared_weight, conv_inner, conv_shared, step_bias, decay_log, skip_gain, attention_out, mamba_out, feed_gain, gate_up, down_weight, output_grad):
    params = tuple((value.astype(jnp.float32) for value in (mix_gain, query_weight, zx_weight, step_weight, shared_weight, conv_inner, conv_shared, step_bias, decay_log, skip_gain, attention_out, mamba_out, feed_gain, gate_up, down_weight)))
    group_tokens = SEQS * SEQ_LEN
    group_count = TOKENS // group_tokens
    inputs = block_input.astype(jnp.float32).reshape(group_count, group_tokens, D)
    cotangents = output_grad.astype(jnp.float32).reshape(group_count, group_tokens, D)

    def one_group(running, element):
        group_in, group_grad = element
        output, pull = jax.vjp(block_forward, group_in, *params)
        gradients = pull(group_grad)
        running = tuple((left + right for left, right in zip(running, gradients[1:])))
        return (running, (output.astype(jnp.bfloat16), gradients[0].astype(jnp.bfloat16)))
    start_totals = tuple((jnp.zeros_like(value) for value in params))
    totals, (outputs, input_grads) = lax.scan(one_group, start_totals, (inputs, cotangents))
    return (outputs.reshape(TOKENS, D), input_grads.reshape(TOKENS, D), totals[0], totals[1], totals[2], totals[3], totals[4], totals[5], totals[6], totals[7], totals[8], totals[9], totals[10], totals[11], totals[12], totals[13], totals[14])
```

```python
import jax
import jax.numpy as jnp
from jax import lax
from jax.experimental import pallas as pl
from jax.experimental.pallas import tpu as pltpu
from jax.sharding import PartitionSpec as P

HEADS = 8
KV_HEADS = 2
HEAD_DIM = 64
SEQ_LEN = 2048
SPAN = 128
STATE = 128
QBLOCK = 512
HALO = 8


epsilon = 1e-06
HIGHEST_PRECISION = lax.Precision.HIGHEST
NEG = -1e30


def rms_norm(values, gain):
    factor = lax.rsqrt(jnp.mean(values * values, axis=-1, keepdims=True) + epsilon)
    return values * factor * gain


def mm(left, right, left_dim, right_dim):
    return lax.dot_general(
        left, right, (((left_dim,), (right_dim,)), ((), ())), preferred_element_type=jnp.float32
    )


def low(values):
    return values.astype(jnp.bfloat16)


def whole(ref_count):
    return [pl.BlockSpec(memory_space=pltpu.VMEM)] * ref_count


def diagonal_mask():
    row = lax.broadcasted_iota(jnp.int32, (QBLOCK, QBLOCK), 0)
    col = lax.broadcasted_iota(jnp.int32, (QBLOCK, QBLOCK), 1)
    return row >= col


def block_rows(index):
    return pl.ds(pl.multiple_of(index * QBLOCK, QBLOCK), QBLOCK)


def attend_forward_kernel(heads, q_ref, kv_ref, out_ref, lse_ref):
    scale = HEAD_DIM ** (-0.5)

    def query_step(qi, unused):
        rows = block_rows(qi)
        for h in range(heads):
            cols = slice(h * HEAD_DIM, (h + 1) * HEAD_DIM)
            query = q_ref[rows, cols] * scale

            def visit(ki, carry, masked):
                top, total, acc = carry
                krows = block_rows(ki)
                scores = mm(query, kv_ref[krows, :HEAD_DIM], 1, 1)
                if masked:
                    scores = jnp.where(diagonal_mask(), scores, NEG)
                new_top = jnp.maximum(top, jnp.max(scores, axis=1, keepdims=True))
                soft = jnp.exp(scores - new_top)
                shrink = jnp.exp(top - new_top)
                total = total * shrink + jnp.sum(soft, axis=1, keepdims=True)
                acc = acc * shrink + mm(low(soft), kv_ref[krows, HEAD_DIM:], 1, 0)
                return new_top, total, acc

            carry = (
                jnp.full((QBLOCK, 1), NEG, jnp.float32),
                jnp.zeros((QBLOCK, 1), jnp.float32),
                jnp.zeros((QBLOCK, HEAD_DIM), jnp.float32),
            )
            carry = lax.fori_loop(0, qi, lambda ki, c: visit(ki, c, False), carry)
            top, total, acc = visit(qi, carry, True)
            out_ref[rows, cols] = low(acc / total)
            lse_ref[rows, h : h + 1] = top + jnp.log(total)
        return unused

    lax.fori_loop(0, q_ref.shape[0] // QBLOCK, query_step, 0)


def attend_forward(query, keyval):
    heads = query.shape[1] // HEAD_DIM
    return pl.pallas_call(
        lambda *refs: attend_forward_kernel(heads, *refs),
        out_shape=(
            jax.ShapeDtypeStruct(query.shape, jnp.bfloat16),
            jax.ShapeDtypeStruct((query.shape[0], heads), jnp.float32),
        ),
        in_specs=whole(2),
        out_specs=tuple(whole(2)),
        compiler_params=pltpu.CompilerParams(vmem_limit_bytes=40 << 20),
        cost_estimate=pl.CostEstimate(
            flops=heads * SEQ_LEN * SEQ_LEN * HEAD_DIM * 4,
            bytes_accessed=4 << 20,
            transcendentals=heads * SEQ_LEN * SEQ_LEN,
        ),
    )(query, keyval)


def attend_backward_kernel(heads, q_ref, kv_ref, out_ref, lse_ref, do_ref, dq_ref, dkv_ref, acc_ref):
    scale = HEAD_DIM ** (-0.5)
    acc_ref[...] = jnp.zeros_like(acc_ref)

    def query_step(qi, unused):
        rows = block_rows(qi)
        for h in range(heads):
            cols = slice(h * HEAD_DIM, (h + 1) * HEAD_DIM)
            query = q_ref[rows, cols] * scale
            grad = do_ref[rows, cols]
            lse = lse_ref[rows, h : h + 1]
            delta = jnp.sum(
                grad.astype(jnp.float32) * out_ref[rows, cols].astype(jnp.float32),
                axis=1,
                keepdims=True,
            )

            def visit(ki, acc, masked):
                krows = block_rows(ki)
                key = kv_ref[krows, :HEAD_DIM]
                scores = mm(query, key, 1, 1)
                if masked:
                    scores = jnp.where(diagonal_mask(), scores, NEG)
                soft = jnp.exp(scores - lse)
                soft_grad = mm(grad, kv_ref[krows, HEAD_DIM:], 1, 1)
                score_grad = low(soft * (soft_grad - delta))
                acc_ref[krows, :HEAD_DIM] += mm(score_grad, query, 0, 0)
                acc_ref[krows, HEAD_DIM:] += mm(low(soft), grad, 0, 0)
                return acc + mm(score_grad, key, 1, 0)

            acc = jnp.zeros((QBLOCK, HEAD_DIM), jnp.float32)
            acc = lax.fori_loop(0, qi, lambda ki, a: visit(ki, a, False), acc)
            dq_ref[rows, cols] = low(visit(qi, acc, True) * scale)
        return unused

    lax.fori_loop(0, q_ref.shape[0] // QBLOCK, query_step, 0)
    dkv_ref[...] = low(acc_ref[...])


def attend_backward(query, keyval, out, lse, grad):
    heads = query.shape[1] // HEAD_DIM
    return pl.pallas_call(
        lambda *refs: attend_backward_kernel(heads, *refs),
        out_shape=(
            jax.ShapeDtypeStruct(query.shape, jnp.bfloat16),
            jax.ShapeDtypeStruct(keyval.shape, jnp.bfloat16),
        ),
        in_specs=whole(5),
        out_specs=tuple(whole(2)),
        scratch_shapes=[pltpu.VMEM(keyval.shape, jnp.float32)],
        compiler_params=pltpu.CompilerParams(vmem_limit_bytes=40 << 20),
        cost_estimate=pl.CostEstimate(
            flops=heads * SEQ_LEN * SEQ_LEN * HEAD_DIM * 10,
            bytes_accessed=6 << 20,
            transcendentals=heads * SEQ_LEN * SEQ_LEN,
        ),
    )(query, keyval, out, lse, grad)


def span_mask():
    row = lax.broadcasted_iota(jnp.int32, (SPAN, SPAN), 0)
    col = lax.broadcasted_iota(jnp.int32, (SPAN, SPAN), 1)
    return row >= col


def conv_of(extended, taps):
    result = extended[HALO - 3 : HALO - 3 + SPAN, :] * taps[0:1, :]
    for k in range(1, 4):
        result = result + extended[HALO - 3 + k : HALO - 3 + k + SPAN, :] * taps[k : k + 1, :]
    return result


def mamba_forward_kernel(
    nh, z_ref, u_ref, cols_ref, rows_ref, taps_ref, skip_ref, gated_ref, y_ref, prior_ref,
    state_ref, halo_ref,
):
    channels = nh * HEAD_DIM

    @pl.when(pl.program_id(0) == 0)
    def _():
        state_ref[...] = jnp.zeros_like(state_ref)
        halo_ref[...] = jnp.zeros_like(halo_ref)

    raw = u_ref[...]
    pre = conv_of(jnp.concatenate([halo_ref[...], raw], axis=0), taps_ref[...])
    halo_ref[...] = raw[SPAN - HALO :, :]
    conv = pre * jax.nn.sigmoid(pre)
    keys = low(conv[:, channels : channels + STATE])
    queries = low(conv[:, channels + STATE :])
    affinity = mm(queries, keys, 1, 1)
    causal = span_mask()
    prior_ref[0] = state_ref[...]
    for h in range(nh):
        part = slice(h * HEAD_DIM, (h + 1) * HEAD_DIM)
        inner = conv[:, part]
        cum = cols_ref[0, :, h : h + 1]
        step = cols_ref[0, :, nh + h : nh + h + 1]
        cum_row = rows_ref[0, h : h + 1, :]
        step_row = rows_ref[0, nh + h : nh + h + 1, :]
        total = cum[SPAN - 1 : SPAN, :]
        within = jnp.exp(jnp.where(causal, cum - cum_row, NEG))
        mixing = affinity * within * step_row
        state = state_ref[part, :]
        y = mm(low(mixing), low(inner), 1, 0)
        y = y + jnp.exp(cum) * mm(queries, low(state), 1, 1)
        y = y + skip_ref[:, part] * inner
        weight = jnp.exp(total - cum) * step
        state_ref[part, :] = jnp.exp(total) * state + mm(low(inner * weight), keys, 0, 0)
        z = z_ref[:, part]
        y_ref[:, part] = y
        gated_ref[:, part] = low(y * (z * jax.nn.sigmoid(z)))


def mamba_forward(z, u, cols, rows, taps, skip):
    tokens, channels = z.shape
    width = u.shape[1]
    nh = channels // HEAD_DIM
    spans = tokens // SPAN
    return pl.pallas_call(
        lambda *refs: mamba_forward_kernel(nh, *refs),
        grid=(spans,),
        in_specs=[
            pl.BlockSpec((SPAN, channels), lambda c: (c, 0)),
            pl.BlockSpec((SPAN, width), lambda c: (c, 0)),
            pl.BlockSpec((1, SPAN, 2 * nh), lambda c: (c, 0, 0)),
            pl.BlockSpec((1, 2 * nh, SPAN), lambda c: (c, 0, 0)),
            pl.BlockSpec((4, width), lambda c: (0, 0)),
            pl.BlockSpec((1, channels), lambda c: (0, 0)),
        ],
        out_specs=(
            pl.BlockSpec((SPAN, channels), lambda c: (c, 0)),
            pl.BlockSpec((SPAN, channels), lambda c: (c, 0)),
            pl.BlockSpec((1, channels, STATE), lambda c: (c, 0, 0)),
        ),
        out_shape=(
            jax.ShapeDtypeStruct((tokens, channels), jnp.bfloat16),
            jax.ShapeDtypeStruct((tokens, channels), jnp.float32),
            jax.ShapeDtypeStruct((spans, channels, STATE), jnp.float32),
        ),
        scratch_shapes=[
            pltpu.VMEM((channels, STATE), jnp.float32),
            pltpu.VMEM((HALO, width), jnp.float32),
        ],
        compiler_params=pltpu.CompilerParams(vmem_limit_bytes=32 << 20),
        cost_estimate=pl.CostEstimate(
            flops=tokens * channels * 1000, bytes_accessed=tokens * channels * 24, transcendentals=0
        ),
    )(z, u, cols, rows, taps, skip)


def mamba_backward_kernel(
    nh, z_ref, u_ref, before_ref, cols_ref, rows_ref, taps_ref, skip_ref, y_ref, prior_ref, dg_ref,
    dz_ref, du_ref, dcols_ref, drows_ref, dtaps_ref, dskip_ref, dstate_ref, halo_ref, dconv_ref,
):
    channels = nh * HEAD_DIM
    step_id = pl.program_id(0)

    @pl.when(step_id == 0)
    def _():
        dstate_ref[...] = jnp.zeros_like(dstate_ref)
        halo_ref[...] = jnp.zeros_like(halo_ref)
        dtaps_ref[...] = jnp.zeros_like(dtaps_ref)
        dskip_ref[...] = jnp.zeros_like(dskip_ref)

    first = step_id == pl.num_programs(0) - 1
    before = jnp.where(first, 0.0, before_ref[...])
    extended = jnp.concatenate([before, u_ref[...]], axis=0)
    taps = taps_ref[...]
    pre = conv_of(extended, taps)
    gate = jax.nn.sigmoid(pre)
    conv = pre * gate
    keys = low(conv[:, channels : channels + STATE])
    queries = low(conv[:, channels + STATE :])
    affinity = mm(queries, keys, 1, 1)
    causal = span_mask()
    last = lax.broadcasted_iota(jnp.int32, (SPAN, 1), 0) == SPAN - 1
    d_affinity = jnp.zeros((SPAN, SPAN), jnp.float32)
    d_keys = jnp.zeros((SPAN, STATE), jnp.float32)
    d_queries = jnp.zeros((SPAN, STATE), jnp.float32)
    for h in range(nh):
        part = slice(h * HEAD_DIM, (h + 1) * HEAD_DIM)
        inner = conv[:, part]
        inner_low = low(inner)
        cum = cols_ref[0, :, h : h + 1]
        step = cols_ref[0, :, nh + h : nh + h + 1]
        cum_row = rows_ref[0, h : h + 1, :]
        step_row = rows_ref[0, nh + h : nh + h + 1, :]
        total = cum[SPAN - 1 : SPAN, :]
        within = jnp.exp(jnp.where(causal, cum - cum_row, NEG))
        state = prior_ref[0, part, :]
        state_low = low(state)
        d_state = dstate_ref[part, :]
        d_state_low = low(d_state)
        z = z_ref[:, part]
        sig = jax.nn.sigmoid(z)
        silu = z * sig
        d_gated = dg_ref[:, part].astype(jnp.float32)
        dz_ref[:, part] = low(d_gated * y_ref[:, part] * (sig * (1.0 + z * (1.0 - sig))))
        dy = d_gated * silu
        dy_low = low(dy)
        dskip_ref[:, part] += jnp.sum(dy * inner, axis=0, keepdims=True)
        mixing_grad = mm(dy_low, inner_low, 1, 1)
        weighted = within * step_row
        d_affinity = d_affinity + mixing_grad * weighted
        shaped = mixing_grad * affinity * within
        spread_grad = shaped * step_row
        d_inner = mm(low(affinity * weighted), dy_low, 0, 0) + skip_ref[:, part] * dy
        growth = jnp.exp(cum)
        carried = dy * growth
        carried_low = low(carried)
        d_cum = jnp.sum(spread_grad, axis=1, keepdims=True) + jnp.sum(
            carried * mm(queries, state_low, 1, 1), axis=1, keepdims=True
        )
        d_queries = d_queries + mm(carried_low, state_low, 1, 0)
        fall = jnp.exp(total - cum)
        weight = fall * step
        fresh_grad = mm(keys, d_state_low, 1, 1)
        d_inner = d_inner + weight * fresh_grad
        d_keys = d_keys + mm(low(inner * weight), d_state_low, 1, 0)
        d_weight = jnp.sum(inner * fresh_grad, axis=1, keepdims=True)
        moved = d_weight * weight
        kept = jnp.exp(total)
        d_total = jnp.sum(moved, axis=0, keepdims=True) + kept * jnp.sum(
            jnp.sum(state * d_state, axis=1, keepdims=True), axis=0, keepdims=True
        )
        dstate_ref[part, :] = kept * d_state + mm(carried_low, queries, 0, 0)
        dcols_ref[0, :, h : h + 1] = d_cum - moved + jnp.where(last, d_total, 0.0)
        dcols_ref[0, :, nh + h : nh + h + 1] = d_weight * fall
        drows_ref[0, h : h + 1, :] = -jnp.sum(spread_grad, axis=0, keepdims=True)
        drows_ref[0, nh + h : nh + h + 1, :] = jnp.sum(shaped, axis=0, keepdims=True)
        dconv_ref[:, part] = d_inner
    d_affinity_low = low(d_affinity)
    dconv_ref[:, channels : channels + STATE] = d_keys + mm(d_affinity_low, queries, 0, 0)
    dconv_ref[:, channels + STATE :] = d_queries + mm(d_affinity_low, keys, 1, 0)
    d_pre = dconv_ref[...] * (gate * (1.0 + pre * (1.0 - gate)))
    after = jnp.concatenate([d_pre, halo_ref[...]], axis=0)
    halo_ref[...] = d_pre[:HALO, :]
    d_raw = after[3 : 3 + SPAN, :] * taps[0:1, :]
    for k in range(1, 4):
        d_raw = d_raw + after[3 - k : 3 - k + SPAN, :] * taps[k : k + 1, :]
    du_ref[...] = low(d_raw)
    for k in range(4):
        shifted = extended[HALO - 3 + k : HALO - 3 + k + SPAN, :]
        dtaps_ref[k : k + 1, :] += jnp.sum(d_pre * shifted, axis=0, keepdims=True)


def mamba_backward(z, u, cols, rows, taps, skip, y, prior, d_gated):
    tokens, channels = z.shape
    width = u.shape[1]
    nh = channels // HEAD_DIM
    spans = tokens // SPAN
    per = SPAN // HALO
    back = lambda i: spans - 1 - i
    token_spec = lambda cols_count: pl.BlockSpec((SPAN, cols_count), lambda i: (back(i), 0))
    cols_spec = pl.BlockSpec((1, SPAN, 2 * nh), lambda i: (back(i), 0, 0))
    rows_spec = pl.BlockSpec((1, 2 * nh, SPAN), lambda i: (back(i), 0, 0))
    taps_spec = pl.BlockSpec((4, width), lambda i: (0, 0))
    skip_spec = pl.BlockSpec((1, channels), lambda i: (0, 0))
    return pl.pallas_call(
        lambda *refs: mamba_backward_kernel(nh, *refs),
        grid=(spans,),
        in_specs=[
            token_spec(channels),
            token_spec(width),
            pl.BlockSpec((HALO, width), lambda i: (jnp.maximum(back(i) * per - 1, 0), 0)),
            cols_spec,
            rows_spec,
            taps_spec,
            skip_spec,
            token_spec(channels),
            pl.BlockSpec((1, channels, STATE), lambda i: (back(i), 0, 0)),
            token_spec(channels),
        ],
        out_specs=(
            token_spec(channels), token_spec(width), cols_spec, rows_spec, taps_spec, skip_spec,
        ),
        out_shape=(
            jax.ShapeDtypeStruct((tokens, channels), jnp.bfloat16),
            jax.ShapeDtypeStruct((tokens, width), jnp.bfloat16),
            jax.ShapeDtypeStruct(cols.shape, jnp.float32),
            jax.ShapeDtypeStruct(rows.shape, jnp.float32),
            jax.ShapeDtypeStruct((4, width), jnp.float32),
            jax.ShapeDtypeStruct((1, channels), jnp.float32),
        ),
        scratch_shapes=[
            pltpu.VMEM((channels, STATE), jnp.float32),
            pltpu.VMEM((HALO, width), jnp.float32),
            pltpu.VMEM((SPAN, width), jnp.float32),
        ],
        compiler_params=pltpu.CompilerParams(vmem_limit_bytes=32 << 20),
        cost_estimate=pl.CostEstimate(
            flops=tokens * channels * 3000, bytes_accessed=tokens * channels * 32, transcendentals=0
        ),
    )(z, u, u, cols, rows, taps, skip, y, prior, d_gated)


def step_tables(step_raw, step_bias, decay_log):
    nh = step_raw.shape[1]
    steps = jax.nn.softplus(step_raw + step_bias).reshape(-1, SPAN, nh)
    position = jnp.arange(SPAN)
    lower = (position[:, None] >= position[None, :]).astype(jnp.float32)
    change = steps * -jnp.exp(decay_log)
    cumulative = jnp.einsum("qr,crh->cqh", lower, change, precision=HIGHEST_PRECISION)
    cols = jnp.concatenate([cumulative, steps], axis=2)
    return cols, jnp.swapaxes(cols, 1, 2)


def local(
    block_input,
    mix_gain,
    query_weight,
    zx_weight,
    step_weight,
    shared_weight,
    conv_inner,
    conv_shared,
    step_bias,
    decay_log,
    skip_gain,
    attention_out,
    mamba_out,
    feed_gain,
    gate_up,
    down_weight,
    output_grad,
):
    rows_here = query_weight.shape[0]
    q_cols = query_weight.shape[1]
    channels = zx_weight.shape[2]
    nh = step_weight.shape[1]
    units = gate_up.shape[2]
    local_heads = q_cols // HEAD_DIM
    group_size = HEADS // KV_HEADS
    kv_owner = lax.axis_index("tp") * local_heads // group_size
    inputs = block_input.astype(jnp.float32)
    normed, norm_pull = jax.vjp(rms_norm, inputs, mix_gain)
    mix_weights = jnp.concatenate(
        [
            query_weight,
            zx_weight.reshape(rows_here, 2 * channels),
            shared_weight.reshape(rows_here, 4 * STATE),
            step_weight,
        ],
        axis=1,
    )
    mix_all = lax.all_gather(mix_weights, "wide", axis=0, tiled=True)
    token_rows = lax.all_gather(low(normed), "tp", axis=0, tiled=True)
    feed_weights = jnp.concatenate(
        [
            attention_out.T,
            mamba_out.T,
            gate_up.reshape(rows_here, 2 * units),
            down_weight.T,
        ],
        axis=1,
    )
    feed_weights, cotangent, token_rows, mix_all = lax.optimization_barrier(
        (feed_weights, output_grad, token_rows, mix_all)
    )
    feed_all = lax.all_gather(feed_weights, "wide", axis=0, tiled=True)
    grad_rows = lax.all_gather(cotangent, "tp", axis=0, tiled=True)
    zx_at = q_cols
    shared_at = zx_at + 2 * channels
    step_at = shared_at + 4 * STATE
    kv_all = mix_all[:, shared_at : shared_at + 2 * STATE].reshape(-1, 2, STATE)
    kv_use = lax.dynamic_slice_in_dim(kv_all, kv_owner * HEAD_DIM, HEAD_DIM, 2).reshape(
        -1, 2 * HEAD_DIM
    )
    attn_weight = jnp.concatenate([mix_all[:, :q_cols], kv_use], axis=1)
    scan_weight = jnp.concatenate(
        [mix_all[:, zx_at:shared_at], mix_all[:, shared_at + 2 * STATE :]], axis=1
    )
    attn_in = low(mm(token_rows, attn_weight, 1, 0))
    query, keyval = attn_in[:, :q_cols], attn_in[:, q_cols:]
    z = mm(token_rows, scan_weight[:, :channels], 1, 0)
    u = mm(token_rows, scan_weight[:, channels : 2 * channels + 2 * STATE], 1, 0)
    step_raw = mm(token_rows, scan_weight[:, 2 * channels + 2 * STATE :], 1, 0)
    (cols, rows), tables_pull = jax.vjp(step_tables, step_raw, step_bias, decay_log)
    taps = jnp.concatenate([conv_inner, conv_shared.reshape(-1, 2 * STATE)], axis=1)
    skip = jnp.repeat(skip_gain, HEAD_DIM)[None, :]
    attn, lse = attend_forward(query, keyval)
    gated, y, prior = mamba_forward(z, u, cols, rows, taps, skip)
    mixer_out = jnp.concatenate([attn, gated], axis=1)
    feed_all, mixer_out, grad_rows = lax.optimization_barrier((feed_all, mixer_out, grad_rows))
    out_width = q_cols + channels
    out_weight = feed_all[:, :out_width]
    gate_up_use = feed_all[:, out_width : out_width + 2 * units]
    down_use = feed_all[:, out_width + 2 * units :]
    mixed = lax.psum_scatter(
        low(mm(mixer_out, out_weight, 1, 1)), "tp", scatter_dimension=0, tiled=True
    ).astype(jnp.float32)
    hidden_grad = mm(grad_rows, down_use, 1, 0)
    hidden_state = inputs + mixed
    normed_two, norm_two_pull = jax.vjp(rms_norm, hidden_state, feed_gain)
    feed_rows = lax.all_gather(low(normed_two), "tp", axis=0, tiled=True)
    gate_vals = mm(feed_rows, gate_up_use, 1, 0)
    gate_part = gate_vals[:, :units]
    up_part = gate_vals[:, units:]
    sigmoid_gate = jax.nn.sigmoid(gate_part)
    silu_gate = gate_part * sigmoid_gate
    hidden_low = low(silu_gate * up_part)
    gate_grad = hidden_grad * up_part * (sigmoid_gate * (1.0 + gate_part * (1.0 - sigmoid_gate)))
    gate_up_low = jnp.concatenate([low(gate_grad), low(hidden_grad * silu_gate)], axis=1)
    normed_two_grad = lax.psum_scatter(
        low(mm(gate_up_low, gate_up_use, 1, 1)), "tp", scatter_dimension=0, tiled=True
    ).astype(jnp.float32)
    feed_part = low(mm(hidden_low, down_use, 1, 1))
    down_term = low(mm(grad_rows, hidden_low, 0, 0))
    gate_up_term = low(mm(feed_rows, gate_up_low, 0, 0))
    state_from_norm, feed_gain_term = norm_two_pull(normed_two_grad)
    state_grad = output_grad.astype(jnp.float32) + state_from_norm
    mixed_rows = lax.all_gather(low(state_grad), "tp", axis=0, tiled=True)
    mixer_grad = low(mm(mixed_rows, out_weight, 1, 0))
    out_term = low(mm(mixed_rows, mixer_out, 0, 0))
    mixer_grad, feed_part, out_term, gate_up_term, down_term = lax.optimization_barrier(
        (mixer_grad, feed_part, out_term, gate_up_term, down_term)
    )
    feed_sum = lax.psum_scatter(
        jnp.concatenate([out_term, gate_up_term, down_term], axis=1),
        "wide",
        scatter_dimension=0,
        tiled=True,
    )
    feed_out = lax.psum_scatter(feed_part, "tp", scatter_dimension=0, tiled=True)
    query_grad, keyval_grad = attend_backward(query, keyval, attn, lse, mixer_grad[:, :q_cols])
    z_grad, u_grad, cols_grad, rows_grad, taps_term, skip_row = mamba_backward(
        z, u, cols, rows, taps, skip, y, prior, mixer_grad[:, q_cols:]
    )
    step_in_grad, step_bias_term, decay_log_term = tables_pull((cols_grad, rows_grad))
    all_grad = jnp.concatenate(
        [query_grad, keyval_grad, z_grad, u_grad, low(step_in_grad)], axis=1
    )
    all_weight = jnp.concatenate([attn_weight, scan_weight], axis=1)
    all_grad, feed_sum, feed_out = lax.optimization_barrier((all_grad, feed_sum, feed_out))
    row_grad = low(mm(all_grad, all_weight, 1, 1))
    normed_grad = lax.psum_scatter(row_grad, "tp", scatter_dimension=0, tiled=True)
    term = low(mm(token_rows, all_grad, 0, 0))
    kv_end = q_cols + 2 * HEAD_DIM
    keyval_placed = lax.dynamic_update_slice_in_dim(
        jnp.zeros((term.shape[0], 2, STATE), jnp.bfloat16),
        term[:, q_cols:kv_end].reshape(-1, 2, HEAD_DIM),
        kv_owner * HEAD_DIM,
        2,
    ).reshape(-1, 2 * STATE)
    mix_term = jnp.concatenate(
        [
            term[:, :q_cols],
            term[:, kv_end : kv_end + 2 * channels],
            keyval_placed,
            term[:, kv_end + 2 * channels :],
        ],
        axis=1,
    )
    mix_sum = lax.psum_scatter(mix_term, "wide", scatter_dimension=0, tiled=True)
    block_output = low(hidden_state + feed_out.astype(jnp.float32))
    input_from_norm, mix_gain_term = norm_pull(normed_grad.astype(jnp.float32))
    input_grad = low(state_grad + input_from_norm)
    skip_term = jnp.sum(skip_row.reshape(nh, HEAD_DIM), axis=1)
    own = jnp.concatenate(
        [taps_term[:, :channels].reshape(-1), step_bias_term, decay_log_term, skip_term]
    )
    common = jnp.concatenate(
        [mix_gain_term, feed_gain_term, taps_term[:, channels:].reshape(-1)]
    )
    small = lax.psum(jnp.concatenate([common, own]), "wide")
    common_count = common.shape[0]
    width = mix_gain.shape[0]
    shared_part = mix_sum[:, shared_at:step_at]
    tp_sum = lax.psum(
        jnp.concatenate([shared_part.reshape(-1), low(small[:common_count])]), "tp"
    ).astype(jnp.float32)
    shared_sum = tp_sum[: shared_part.size].reshape(rows_here, 4, STATE)
    common_sum = tp_sum[shared_part.size :]
    own_sum = small[common_count:]
    taps_count = conv_inner.size
    mix_sum = mix_sum.astype(jnp.float32)
    feed_sum = feed_sum.astype(jnp.float32)
    return (
        block_output,
        input_grad,
        common_sum[:width],
        mix_sum[:, :q_cols],
        mix_sum[:, zx_at:shared_at].reshape(rows_here, 2, channels),
        mix_sum[:, step_at:],
        shared_sum,
        own_sum[:taps_count].reshape(conv_inner.shape),
        common_sum[2 * width :].reshape(conv_shared.shape),
        own_sum[taps_count : taps_count + nh],
        own_sum[taps_count + nh : taps_count + 2 * nh],
        own_sum[taps_count + 2 * nh :],
        feed_sum[:, :q_cols].T,
        feed_sum[:, q_cols:out_width].T,
        common_sum[width : 2 * width],
        feed_sum[:, out_width : out_width + 2 * units].reshape(rows_here, 2, units),
        feed_sum[:, out_width + 2 * units :].T,
    )


def solution(mesh):
    placed = (
        P(("wide", "tp"), None),
        P(),
        P("wide", "tp"),
        P("wide", None, "tp"),
        P("wide", "tp"),
        P("wide", None, None),
        P(None, "tp"),
        P(),
        P("tp"),
        P("tp"),
        P("tp"),
        P("tp", "wide"),
        P("tp", "wide"),
        P(),
        P("wide", None, "tp"),
        P("tp", "wide"),
        P(("wide", "tp"), None),
    )
    return jax.shard_map(
        local,
        mesh=mesh,
        in_specs=placed,
        out_specs=(
            P(("wide", "tp"), None),
            P(("wide", "tp"), None),
            P(),
            P("wide", "tp"),
            P("wide", None, "tp"),
            P("wide", "tp"),
            P("wide", None, None),
            P(None, "tp"),
            P(),
            P("tp"),
            P("tp"),
            P("tp"),
            P("tp", "wide"),
            P("tp", "wide"),
            P(),
            P("wide", None, "tp"),
            P("tp", "wide"),
        ),
        check_vma=False,
    )
```

```python
import jax
import jax.numpy as jnp
from jax import lax
from jax.experimental import pallas as pl
from jax.experimental.pallas import tpu as pltpu
from jax.sharding import PartitionSpec as P

HEADS = 8
KV_HEADS = 2
HEAD_DIM = 64
SEQ_LEN = 2048
SPAN = 128
STATE = 128
QBLOCK = 512
HALO = 8


epsilon = 1e-06
HIGHEST_PRECISION = lax.Precision.HIGHEST
NEG = -1e30


def rms_norm(values, gain):
    factor = lax.rsqrt(jnp.mean(values * values, axis=-1, keepdims=True) + epsilon)
    return values * factor * gain


def mm(left, right, left_dim, right_dim):
    return lax.dot_general(
        left, right, (((left_dim,), (right_dim,)), ((), ())), preferred_element_type=jnp.float32
    )


def low(values):
    return values.astype(jnp.bfloat16)


def whole(ref_count):
    return [pl.BlockSpec(memory_space=pltpu.VMEM)] * ref_count


def diagonal_mask():
    row = lax.broadcasted_iota(jnp.int32, (QBLOCK, QBLOCK), 0)
    col = lax.broadcasted_iota(jnp.int32, (QBLOCK, QBLOCK), 1)
    return row <= col


def block_rows(index):
    return pl.ds(pl.multiple_of(index * QBLOCK, QBLOCK), QBLOCK)


def attend_forward_kernel(heads, q_ref, k_ref, vt_ref, out_ref, lse_ref):
    scale = HEAD_DIM ** (-0.5)

    def query_step(qi, unused):
        cols = block_rows(qi)
        for h in range(heads):
            part = slice(h * HEAD_DIM, (h + 1) * HEAD_DIM)
            query = q_ref[cols, part] * scale

            def visit(ki, carry, masked):
                top, total, acc = carry
                krows = block_rows(ki)
                scores = mm(k_ref[krows, :], query, 1, 1)
                if masked:
                    scores = jnp.where(diagonal_mask(), scores, NEG)
                new_top = jnp.maximum(top, jnp.max(scores, axis=0, keepdims=True))
                soft = jnp.exp(scores - new_top)
                shrink = jnp.exp(top - new_top)
                total = total * shrink + jnp.sum(soft, axis=0, keepdims=True)
                acc = acc * shrink + mm(vt_ref[:, krows], low(soft), 1, 0)
                return new_top, total, acc

            carry = (
                jnp.full((1, QBLOCK), NEG, jnp.float32),
                jnp.zeros((1, QBLOCK), jnp.float32),
                jnp.zeros((HEAD_DIM, QBLOCK), jnp.float32),
            )
            carry = lax.fori_loop(0, qi, lambda ki, c: visit(ki, c, False), carry)
            top, total, acc = visit(qi, carry, True)
            out_ref[part, cols] = low(acc / total)
            lse_ref[h : h + 1, cols] = top + jnp.log(total)
        return unused

    lax.fori_loop(0, q_ref.shape[0] // QBLOCK, query_step, 0)


def attend_forward(query, keyval):
    tokens, width = query.shape
    heads = width // HEAD_DIM
    out, lse = pl.pallas_call(
        lambda *refs: attend_forward_kernel(heads, *refs),
        out_shape=(
            jax.ShapeDtypeStruct((width, tokens), jnp.bfloat16),
            jax.ShapeDtypeStruct((heads, tokens), jnp.float32),
        ),
        in_specs=whole(3),
        out_specs=tuple(whole(2)),
        compiler_params=pltpu.CompilerParams(vmem_limit_bytes=40 << 20),
        cost_estimate=pl.CostEstimate(
            flops=heads * SEQ_LEN * SEQ_LEN * HEAD_DIM * 4,
            bytes_accessed=4 << 20,
            transcendentals=heads * SEQ_LEN * SEQ_LEN,
        ),
    )(query, keyval[:, :HEAD_DIM], keyval[:, HEAD_DIM:].T)
    return out.T, lse


def attend_backward_kernel(
    heads, q_ref, k_ref, kt_ref, v_ref, lse_ref, delta_ref, do_ref, dq_ref, dkv_ref, acc_ref
):
    scale = HEAD_DIM ** (-0.5)
    acc_ref[...] = jnp.zeros_like(acc_ref)

    def query_step(qi, unused):
        cols = block_rows(qi)
        for h in range(heads):
            part = slice(h * HEAD_DIM, (h + 1) * HEAD_DIM)
            query = q_ref[cols, part] * scale
            grad = do_ref[cols, part]
            lse = lse_ref[h : h + 1, cols]
            delta = delta_ref[h : h + 1, cols]

            def visit(ki, acc, masked):
                krows = block_rows(ki)
                scores = mm(k_ref[krows, :], query, 1, 1)
                if masked:
                    scores = jnp.where(diagonal_mask(), scores, NEG)
                soft = jnp.exp(scores - lse)
                soft_grad = mm(v_ref[krows, :], grad, 1, 1)
                score_grad = low(soft * (soft_grad - delta))
                acc_ref[krows, :HEAD_DIM] += mm(score_grad, query, 1, 0)
                acc_ref[krows, HEAD_DIM:] += mm(low(soft), grad, 1, 0)
                return acc + mm(kt_ref[:, krows], score_grad, 1, 0)

            acc = jnp.zeros((HEAD_DIM, QBLOCK), jnp.float32)
            acc = lax.fori_loop(0, qi, lambda ki, a: visit(ki, a, False), acc)
            dq_ref[part, cols] = low(visit(qi, acc, True) * scale)
        return unused

    lax.fori_loop(0, q_ref.shape[0] // QBLOCK, query_step, 0)
    dkv_ref[...] = low(acc_ref[...])


def attend_backward(query, keyval, out, lse, grad):
    tokens, width = query.shape
    heads = width // HEAD_DIM
    product = grad.astype(jnp.float32) * out.astype(jnp.float32)
    delta = jnp.sum(product.reshape(tokens, heads, HEAD_DIM), axis=2).T
    key = keyval[:, :HEAD_DIM]
    query_grad, keyval_grad = pl.pallas_call(
        lambda *refs: attend_backward_kernel(heads, *refs),
        out_shape=(
            jax.ShapeDtypeStruct((width, tokens), jnp.bfloat16),
            jax.ShapeDtypeStruct(keyval.shape, jnp.bfloat16),
        ),
        in_specs=whole(7),
        out_specs=tuple(whole(2)),
        scratch_shapes=[pltpu.VMEM(keyval.shape, jnp.float32)],
        compiler_params=pltpu.CompilerParams(vmem_limit_bytes=40 << 20),
        cost_estimate=pl.CostEstimate(
            flops=heads * SEQ_LEN * SEQ_LEN * HEAD_DIM * 10,
            bytes_accessed=6 << 20,
            transcendentals=heads * SEQ_LEN * SEQ_LEN,
        ),
    )(query, key, key.T, keyval[:, HEAD_DIM:], lse, delta, grad)
    return query_grad.T, keyval_grad


def span_mask():
    row = lax.broadcasted_iota(jnp.int32, (SPAN, SPAN), 0)
    col = lax.broadcasted_iota(jnp.int32, (SPAN, SPAN), 1)
    return row >= col


def conv_of(extended, taps):
    result = extended[HALO - 3 : HALO - 3 + SPAN, :] * taps[0:1, :]
    for k in range(1, 4):
        result = result + extended[HALO - 3 + k : HALO - 3 + k + SPAN, :] * taps[k : k + 1, :]
    return result


def mamba_forward_kernel(
    nh, z_ref, u_ref, cols_ref, rows_ref, taps_ref, skip_ref, gated_ref, y_ref, prior_ref,
    state_ref, halo_ref,
):
    channels = nh * HEAD_DIM

    @pl.when(pl.program_id(0) == 0)
    def _():
        state_ref[...] = jnp.zeros_like(state_ref)
        halo_ref[...] = jnp.zeros_like(halo_ref)

    raw = u_ref[...]
    pre = conv_of(jnp.concatenate([halo_ref[...], raw], axis=0), taps_ref[...])
    halo_ref[...] = raw[SPAN - HALO :, :]
    conv = pre * jax.nn.sigmoid(pre)
    keys = low(conv[:, channels : channels + STATE])
    queries = low(conv[:, channels + STATE :])
    affinity = mm(queries, keys, 1, 1)
    causal = span_mask()
    prior_ref[0] = state_ref[...]
    for h in range(nh):
        part = slice(h * HEAD_DIM, (h + 1) * HEAD_DIM)
        inner = conv[:, part]
        cum = cols_ref[0, :, h : h + 1]
        step = cols_ref[0, :, nh + h : nh + h + 1]
        cum_row = rows_ref[0, h : h + 1, :]
        step_row = rows_ref[0, nh + h : nh + h + 1, :]
        total = cum[SPAN - 1 : SPAN, :]
        within = jnp.exp(jnp.where(causal, cum - cum_row, NEG))
        mixing = affinity * within * step_row
        state = state_ref[part, :]
        y = mm(low(mixing), low(inner), 1, 0)
        y = y + jnp.exp(cum) * mm(queries, low(state), 1, 1)
        y = y + skip_ref[:, part] * inner
        weight = jnp.exp(total - cum) * step
        state_ref[part, :] = jnp.exp(total) * state + mm(low(inner * weight), keys, 0, 0)
        z = z_ref[:, part]
        y_ref[:, part] = y
        gated_ref[:, part] = low(y * (z * jax.nn.sigmoid(z)))


def mamba_forward(z, u, cols, rows, taps, skip):
    tokens, channels = z.shape
    width = u.shape[1]
    nh = channels // HEAD_DIM
    spans = tokens // SPAN
    return pl.pallas_call(
        lambda *refs: mamba_forward_kernel(nh, *refs),
        grid=(spans,),
        in_specs=[
            pl.BlockSpec((SPAN, channels), lambda c: (c, 0)),
            pl.BlockSpec((SPAN, width), lambda c: (c, 0)),
            pl.BlockSpec((1, SPAN, 2 * nh), lambda c: (c, 0, 0)),
            pl.BlockSpec((1, 2 * nh, SPAN), lambda c: (c, 0, 0)),
            pl.BlockSpec((4, width), lambda c: (0, 0)),
            pl.BlockSpec((1, channels), lambda c: (0, 0)),
        ],
        out_specs=(
            pl.BlockSpec((SPAN, channels), lambda c: (c, 0)),
            pl.BlockSpec((SPAN, channels), lambda c: (c, 0)),
            pl.BlockSpec((1, channels, STATE), lambda c: (c, 0, 0)),
        ),
        out_shape=(
            jax.ShapeDtypeStruct((tokens, channels), jnp.bfloat16),
            jax.ShapeDtypeStruct((tokens, channels), jnp.float32),
            jax.ShapeDtypeStruct((spans, channels, STATE), jnp.float32),
        ),
        scratch_shapes=[
            pltpu.VMEM((channels, STATE), jnp.float32),
            pltpu.VMEM((HALO, width), jnp.float32),
        ],
        compiler_params=pltpu.CompilerParams(vmem_limit_bytes=32 << 20),
        cost_estimate=pl.CostEstimate(
            flops=tokens * channels * 1000, bytes_accessed=tokens * channels * 24, transcendentals=0
        ),
    )(z, u, cols, rows, taps, skip)


def mamba_backward_kernel(
    nh, z_ref, u_ref, before_ref, cols_ref, rows_ref, wide_ref, taps_ref, skip_ref, y_ref, prior_ref,
    dg_ref, dz_ref, du_ref, dcols_ref, drows_ref, dwide_ref, dtaps_ref, dskip_ref, dstate_ref,
    halo_ref, dconv_ref,
):
    channels = nh * HEAD_DIM
    step_id = pl.program_id(0)

    @pl.when(step_id == 0)
    def _():
        dstate_ref[...] = jnp.zeros_like(dstate_ref)
        halo_ref[...] = jnp.zeros_like(halo_ref)
        dtaps_ref[...] = jnp.zeros_like(dtaps_ref)
        dskip_ref[...] = jnp.zeros_like(dskip_ref)

    first = step_id == pl.num_programs(0) - 1
    before = jnp.where(first, 0.0, before_ref[...])
    extended = jnp.concatenate([before, u_ref[...]], axis=0)
    taps = taps_ref[...]
    pre = conv_of(extended, taps)
    gate = jax.nn.sigmoid(pre)
    conv = pre * gate
    keys = low(conv[:, channels : channels + STATE])
    queries = low(conv[:, channels + STATE :])
    affinity = mm(queries, keys, 1, 1)
    causal = span_mask()
    last = lax.broadcasted_iota(jnp.int32, (SPAN, 1), 0) == SPAN - 1
    d_affinity = jnp.zeros((SPAN, SPAN), jnp.float32)
    inner = conv[:, :channels]
    inner_low = low(inner)
    state = prior_ref[0]
    state_low = low(state)
    d_state = dstate_ref[...]
    d_state_low = low(d_state)
    z = z_ref[...]
    sig = jax.nn.sigmoid(z)
    d_gated = dg_ref[...].astype(jnp.float32)
    dz_ref[...] = low(d_gated * y_ref[...] * (sig * (1.0 + z * (1.0 - sig))))
    dy = d_gated * (z * sig)
    dy_low = low(dy)
    dskip_ref[...] += jnp.sum(dy * inner, axis=0, keepdims=True)
    cum_wide = wide_ref[:, :channels]
    step_wide = wide_ref[:, channels:]
    carried = dy * jnp.exp(cum_wide)
    carried_low = low(carried)
    fall_wide = jnp.exp(cum_wide[SPAN - 1 : SPAN, :] - cum_wide)
    weight = fall_wide * step_wide
    fresh_grad = mm(keys, d_state_low, 1, 1)
    d_weight = inner * fresh_grad
    moved = d_weight * weight
    dwide_ref[:, :channels] = (
        carried * mm(queries, state_low, 1, 1)
        - moved
        + jnp.where(last, jnp.sum(moved, axis=0, keepdims=True), 0.0)
    )
    dwide_ref[:, channels:] = d_weight * fall_wide
    d_queries = mm(carried_low, state_low, 1, 0)
    d_keys = mm(low(inner * weight), d_state_low, 1, 0)
    d_state_in = mm(carried_low, queries, 0, 0)
    dconv_ref[:, :channels] = weight * fresh_grad + skip_ref[...] * dy
    for h in range(nh):
        part = slice(h * HEAD_DIM, (h + 1) * HEAD_DIM)
        cum = cols_ref[0, :, h : h + 1]
        cum_row = rows_ref[0, h : h + 1, :]
        step_row = rows_ref[0, nh + h : nh + h + 1, :]
        within = jnp.exp(jnp.where(causal, cum - cum_row, NEG))
        mixing_grad = mm(dy_low[:, part], inner_low[:, part], 1, 1)
        weighted = within * step_row
        d_affinity = d_affinity + mixing_grad * weighted
        shaped = mixing_grad * affinity * within
        spread_grad = shaped * step_row
        dconv_ref[:, part] += mm(low(affinity * weighted), dy_low[:, part], 0, 0)
        kept = jnp.exp(cum[SPAN - 1 : SPAN, :])
        d_total = kept * jnp.sum(
            jnp.sum(state[part, :] * d_state[part, :], axis=0, keepdims=True), axis=1, keepdims=True
        )
        dstate_ref[part, :] = kept * d_state[part, :] + d_state_in[part, :]
        dcols_ref[0, :, h : h + 1] = jnp.sum(spread_grad, axis=1, keepdims=True) + jnp.where(
            last, d_total, 0.0
        )
        dcols_ref[0, :, nh + h : nh + h + 1] = jnp.zeros((SPAN, 1), jnp.float32)
        drows_ref[0, h : h + 1, :] = -jnp.sum(spread_grad, axis=0, keepdims=True)
        drows_ref[0, nh + h : nh + h + 1, :] = jnp.sum(shaped, axis=0, keepdims=True)
    d_affinity_low = low(d_affinity)
    dconv_ref[:, channels : channels + STATE] = d_keys + mm(d_affinity_low, queries, 0, 0)
    dconv_ref[:, channels + STATE :] = d_queries + mm(d_affinity_low, keys, 1, 0)
    d_pre = dconv_ref[...] * (gate * (1.0 + pre * (1.0 - gate)))
    after = jnp.concatenate([d_pre, halo_ref[...]], axis=0)
    halo_ref[...] = d_pre[:HALO, :]
    d_raw = after[3 : 3 + SPAN, :] * taps[0:1, :]
    for k in range(1, 4):
        d_raw = d_raw + after[3 - k : 3 - k + SPAN, :] * taps[k : k + 1, :]
    du_ref[...] = low(d_raw)
    for k in range(4):
        shifted = extended[HALO - 3 + k : HALO - 3 + k + SPAN, :]
        dtaps_ref[k : k + 1, :] += jnp.sum(d_pre * shifted, axis=0, keepdims=True)


def mamba_backward(z, u, cols, rows, wide, taps, skip, y, prior, d_gated):
    tokens, channels = z.shape
    width = u.shape[1]
    nh = channels // HEAD_DIM
    spans = tokens // SPAN
    per = SPAN // HALO
    back = lambda i: spans - 1 - i
    token_spec = lambda cols_count: pl.BlockSpec((SPAN, cols_count), lambda i: (back(i), 0))
    cols_spec = pl.BlockSpec((1, SPAN, 2 * nh), lambda i: (back(i), 0, 0))
    rows_spec = pl.BlockSpec((1, 2 * nh, SPAN), lambda i: (back(i), 0, 0))
    taps_spec = pl.BlockSpec((4, width), lambda i: (0, 0))
    skip_spec = pl.BlockSpec((1, channels), lambda i: (0, 0))
    return pl.pallas_call(
        lambda *refs: mamba_backward_kernel(nh, *refs),
        grid=(spans,),
        in_specs=[
            token_spec(channels),
            token_spec(width),
            pl.BlockSpec((HALO, width), lambda i: (jnp.maximum(back(i) * per - 1, 0), 0)),
            cols_spec,
            rows_spec,
            token_spec(2 * channels),
            taps_spec,
            skip_spec,
            token_spec(channels),
            pl.BlockSpec((1, channels, STATE), lambda i: (back(i), 0, 0)),
            token_spec(channels),
        ],
        out_specs=(
            token_spec(channels), token_spec(width), cols_spec, rows_spec,
            token_spec(2 * channels), taps_spec, skip_spec,
        ),
        out_shape=(
            jax.ShapeDtypeStruct((tokens, channels), jnp.bfloat16),
            jax.ShapeDtypeStruct((tokens, width), jnp.bfloat16),
            jax.ShapeDtypeStruct(cols.shape, jnp.float32),
            jax.ShapeDtypeStruct(rows.shape, jnp.float32),
            jax.ShapeDtypeStruct(wide.shape, jnp.float32),
            jax.ShapeDtypeStruct((4, width), jnp.float32),
            jax.ShapeDtypeStruct((1, channels), jnp.float32),
        ),
        scratch_shapes=[
            pltpu.VMEM((channels, STATE), jnp.float32),
            pltpu.VMEM((HALO, width), jnp.float32),
            pltpu.VMEM((SPAN, width), jnp.float32),
        ],
        compiler_params=pltpu.CompilerParams(vmem_limit_bytes=32 << 20),
        cost_estimate=pl.CostEstimate(
            flops=tokens * channels * 3000, bytes_accessed=tokens * channels * 32, transcendentals=0
        ),
    )(z, u, u, cols, rows, wide, taps, skip, y, prior, d_gated)


def step_tables(step_raw, step_bias, decay_log):
    nh = step_raw.shape[1]
    steps = jax.nn.softplus(step_raw + step_bias).reshape(-1, SPAN, nh)
    position = jnp.arange(SPAN)
    lower = (position[:, None] >= position[None, :]).astype(jnp.float32)
    change = steps * -jnp.exp(decay_log)
    cumulative = jnp.einsum("qr,crh->cqh", lower, change, precision=HIGHEST_PRECISION)
    cols = jnp.concatenate([cumulative, steps], axis=2)
    wide = jnp.repeat(cols.reshape(-1, 2 * nh), HEAD_DIM, axis=1)
    return cols, jnp.swapaxes(cols, 1, 2), wide


def swap(values, axis, distance):
    size = lax.axis_size(axis)
    return lax.ppermute(values, axis, [(i, i ^ distance) for i in range(size)])


def total_over(values, axis):
    distance = 1
    while distance < lax.axis_size(axis):
        values = values + swap(values, axis, distance)
        distance *= 2
    return values


def gather_tokens(values):
    if lax.axis_size("tp") != 4:
        return lax.all_gather(values, "tp", axis=0, tiled=True)
    count = values.shape[0]
    across = swap(values, "tp", 2)
    beside = swap(values, "tp", 1)
    corner = swap(across, "tp", 1)
    me = lax.axis_index("tp")
    result = jnp.zeros((4 * count, values.shape[1]), values.dtype)
    for distance, piece in ((0, values), (1, beside), (2, across), (3, corner)):
        place = jnp.bitwise_xor(me, distance) * count
        result = lax.dynamic_update_slice_in_dim(result, piece, place, 0)
    return result


def scatter_tokens(values):
    if lax.axis_size("tp") != 4:
        return lax.psum_scatter(values, "tp", scatter_dimension=0, tiled=True).astype(jnp.float32)
    count = values.shape[0] // 4
    me = lax.axis_index("tp")

    def share(distance):
        place = jnp.bitwise_xor(me, distance) * count
        return lax.dynamic_slice_in_dim(values, place, count, 0)

    far = share(2).astype(jnp.float32) + swap(share(3), "tp", 1).astype(jnp.float32)
    near = share(0).astype(jnp.float32) + swap(share(1), "tp", 1).astype(jnp.float32)
    return near + swap(low(far), "tp", 2).astype(jnp.float32)


def local(
    block_input,
    mix_gain,
    query_weight,
    zx_weight,
    step_weight,
    shared_weight,
    conv_inner,
    conv_shared,
    step_bias,
    decay_log,
    skip_gain,
    attention_out,
    mamba_out,
    feed_gain,
    gate_up,
    down_weight,
    output_grad,
):
    rows_here = query_weight.shape[0]
    q_cols = query_weight.shape[1]
    channels = zx_weight.shape[2]
    nh = step_weight.shape[1]
    units = gate_up.shape[2]
    local_heads = q_cols // HEAD_DIM
    group_size = HEADS // KV_HEADS
    kv_owner = lax.axis_index("tp") * local_heads // group_size
    inputs = block_input.astype(jnp.float32)
    normed, norm_pull = jax.vjp(rms_norm, inputs, mix_gain)
    mix_weights = jnp.concatenate(
        [
            query_weight,
            zx_weight.reshape(rows_here, 2 * channels),
            shared_weight.reshape(rows_here, 4 * STATE),
            step_weight,
        ],
        axis=1,
    )
    mix_all = lax.all_gather(mix_weights, "wide", axis=0, tiled=True)
    token_rows = gather_tokens(low(normed))
    feed_weights = jnp.concatenate(
        [
            attention_out.T,
            mamba_out.T,
            gate_up.reshape(rows_here, 2 * units),
            down_weight.T,
        ],
        axis=1,
    )
    feed_weights, cotangent, token_rows, mix_all = lax.optimization_barrier(
        (feed_weights, output_grad, token_rows, mix_all)
    )
    feed_all = lax.all_gather(feed_weights, "wide", axis=0, tiled=True)
    grad_rows = gather_tokens(cotangent)
    zx_at = q_cols
    shared_at = zx_at + 2 * channels
    step_at = shared_at + 4 * STATE
    kv_all = mix_all[:, shared_at : shared_at + 2 * STATE].reshape(-1, 2, STATE)
    kv_use = lax.dynamic_slice_in_dim(kv_all, kv_owner * HEAD_DIM, HEAD_DIM, 2).reshape(
        -1, 2 * HEAD_DIM
    )
    attn_weight = jnp.concatenate([mix_all[:, :q_cols], kv_use], axis=1)
    scan_weight = jnp.concatenate(
        [mix_all[:, zx_at:shared_at], mix_all[:, shared_at + 2 * STATE :]], axis=1
    )
    attn_in = low(mm(token_rows, attn_weight, 1, 0))
    query, keyval = attn_in[:, :q_cols], attn_in[:, q_cols:]
    z = mm(token_rows, scan_weight[:, :channels], 1, 0)
    u = mm(token_rows, scan_weight[:, channels : 2 * channels + 2 * STATE], 1, 0)
    step_raw = mm(token_rows, scan_weight[:, 2 * channels + 2 * STATE :], 1, 0)
    (cols, rows, wide), tables_pull = jax.vjp(step_tables, step_raw, step_bias, decay_log)
    taps = jnp.concatenate([conv_inner, conv_shared.reshape(-1, 2 * STATE)], axis=1)
    skip = jnp.repeat(skip_gain, HEAD_DIM)[None, :]
    attn, lse = attend_forward(query, keyval)
    gated, y, prior = mamba_forward(z, u, cols, rows, taps, skip)
    mixer_out = jnp.concatenate([attn, gated], axis=1)
    feed_all, mixer_out, grad_rows = lax.optimization_barrier((feed_all, mixer_out, grad_rows))
    out_width = q_cols + channels
    out_weight = feed_all[:, :out_width]
    gate_up_use = feed_all[:, out_width : out_width + 2 * units]
    down_use = feed_all[:, out_width + 2 * units :]
    mixed = scatter_tokens(low(mm(mixer_out, out_weight, 1, 1)))
    hidden_grad = mm(grad_rows, down_use, 1, 0)
    hidden_state = inputs + mixed
    normed_two, norm_two_pull = jax.vjp(rms_norm, hidden_state, feed_gain)
    feed_rows = lax.all_gather(low(normed_two), "tp", axis=0, tiled=True)
    gate_vals = mm(feed_rows, gate_up_use, 1, 0)
    gate_part = gate_vals[:, :units]
    up_part = gate_vals[:, units:]
    sigmoid_gate = jax.nn.sigmoid(gate_part)
    silu_gate = gate_part * sigmoid_gate
    hidden_low = low(silu_gate * up_part)
    gate_grad = hidden_grad * up_part * (sigmoid_gate * (1.0 + gate_part * (1.0 - sigmoid_gate)))
    gate_up_low = jnp.concatenate([low(gate_grad), low(hidden_grad * silu_gate)], axis=1)
    normed_two_grad = scatter_tokens(low(mm(gate_up_low, gate_up_use, 1, 1)))
    feed_part = low(mm(hidden_low, down_use, 1, 1))
    down_term = low(mm(grad_rows, hidden_low, 0, 0))
    gate_up_term = low(mm(feed_rows, gate_up_low, 0, 0))
    state_from_norm, feed_gain_term = norm_two_pull(normed_two_grad)
    state_grad = output_grad.astype(jnp.float32) + state_from_norm
    mixed_rows = lax.all_gather(low(state_grad), "tp", axis=0, tiled=True)
    mixer_grad = low(mm(mixed_rows, out_weight, 1, 0))
    out_term = low(mm(mixed_rows, mixer_out, 0, 0))
    mixer_grad, feed_part, out_term, gate_up_term, down_term = lax.optimization_barrier(
        (mixer_grad, feed_part, out_term, gate_up_term, down_term)
    )
    feed_sum = lax.psum_scatter(
        jnp.concatenate([out_term, gate_up_term, down_term], axis=1),
        "wide",
        scatter_dimension=0,
        tiled=True,
    )
    feed_out = scatter_tokens(feed_part)
    query_grad, keyval_grad = attend_backward(query, keyval, attn, lse, mixer_grad[:, :q_cols])
    z_grad, u_grad, cols_grad, rows_grad, wide_grad, taps_term, skip_row = mamba_backward(
        z, u, cols, rows, wide, taps, skip, y, prior, mixer_grad[:, q_cols:]
    )
    step_in_grad, step_bias_term, decay_log_term = tables_pull((cols_grad, rows_grad, wide_grad))
    all_grad = jnp.concatenate(
        [query_grad, keyval_grad, z_grad, u_grad, low(step_in_grad)], axis=1
    )
    all_weight = jnp.concatenate([attn_weight, scan_weight], axis=1)
    all_grad, feed_sum, feed_out = lax.optimization_barrier((all_grad, feed_sum, feed_out))
    row_grad = low(mm(all_grad, all_weight, 1, 1))
    normed_grad = scatter_tokens(row_grad)
    term = low(mm(token_rows, all_grad, 0, 0))
    kv_end = q_cols + 2 * HEAD_DIM
    keyval_placed = lax.dynamic_update_slice_in_dim(
        jnp.zeros((term.shape[0], 2, STATE), jnp.bfloat16),
        term[:, q_cols:kv_end].reshape(-1, 2, HEAD_DIM),
        kv_owner * HEAD_DIM,
        2,
    ).reshape(-1, 2 * STATE)
    mix_term = jnp.concatenate(
        [
            term[:, :q_cols],
            term[:, kv_end : kv_end + 2 * channels],
            keyval_placed,
            term[:, kv_end + 2 * channels :],
        ],
        axis=1,
    )
    mix_sum = lax.psum_scatter(mix_term, "wide", scatter_dimension=0, tiled=True)
    block_output = low(hidden_state + feed_out)
    input_from_norm, mix_gain_term = norm_pull(normed_grad)
    input_grad = low(state_grad + input_from_norm)
    skip_term = jnp.sum(skip_row.reshape(nh, HEAD_DIM), axis=1)
    own = jnp.concatenate(
        [taps_term[:, :channels].reshape(-1), step_bias_term, decay_log_term, skip_term]
    )
    common = jnp.concatenate(
        [mix_gain_term, feed_gain_term, taps_term[:, channels:].reshape(-1)]
    )
    small = total_over(jnp.concatenate([common, own]), "wide")
    common_count = common.shape[0]
    width = mix_gain.shape[0]
    shared_part = mix_sum[:, shared_at:step_at]
    shared_sum = total_over(shared_part.astype(jnp.float32), "tp").reshape(rows_here, 4, STATE)
    common_sum = total_over(small[:common_count], "tp")
    own_sum = small[common_count:]
    taps_count = conv_inner.size
    mix_sum = mix_sum.astype(jnp.float32)
    feed_sum = feed_sum.astype(jnp.float32)
    return (
        block_output,
        input_grad,
        common_sum[:width],
        mix_sum[:, :q_cols],
        mix_sum[:, zx_at:shared_at].reshape(rows_here, 2, channels),
        mix_sum[:, step_at:],
        shared_sum,
        own_sum[:taps_count].reshape(conv_inner.shape),
        common_sum[2 * width :].reshape(conv_shared.shape),
        own_sum[taps_count : taps_count + nh],
        own_sum[taps_count + nh : taps_count + 2 * nh],
        own_sum[taps_count + 2 * nh :],
        feed_sum[:, :q_cols].T,
        feed_sum[:, q_cols:out_width].T,
        common_sum[width : 2 * width],
        feed_sum[:, out_width : out_width + 2 * units].reshape(rows_here, 2, units),
        feed_sum[:, out_width + 2 * units :].T,
    )


def solution(mesh):
    placed = (
        P(("wide", "tp"), None),
        P(),
        P("wide", "tp"),
        P("wide", None, "tp"),
        P("wide", "tp"),
        P("wide", None, None),
        P(None, "tp"),
        P(),
        P("tp"),
        P("tp"),
        P("tp"),
        P("tp", "wide"),
        P("tp", "wide"),
        P(),
        P("wide", None, "tp"),
        P("tp", "wide"),
        P(("wide", "tp"), None),
    )
    return jax.shard_map(
        local,
        mesh=mesh,
        in_specs=placed,
        out_specs=(
            P(("wide", "tp"), None),
            P(("wide", "tp"), None),
            P(),
            P("wide", "tp"),
            P("wide", None, "tp"),
            P("wide", "tp"),
            P("wide", None, None),
            P(None, "tp"),
            P(),
            P("tp"),
            P("tp"),
            P("tp"),
            P("tp", "wide"),
            P("tp", "wide"),
            P(),
            P("wide", None, "tp"),
            P("tp", "wide"),
        ),
        check_vma=False,
    )
```
